512 devices in a mesh: samp: 64 (over z, x), var: 8 (over y, core).
Axes of the slice: x: 4, y: 4, z: 16, core: 2. Of those that a mesh axis runs over, the one named last changes fastest.
Arguments:
- genotypes: bfloat16 [32768, 32768], P('samp', 'var'), may hold values from 0 to 2
- frequency: float32 [32768], P('var'), may hold values from 0.05 to 0.5
- start_block: float32 [32768, 16], P('var'), may hold values from -6 to 6
Outputs:
- loadings: float32 [32768, 16], P('var')
- scores: float32 [32768, 16], P('samp')
The draws below stay inside these ranges and needn't reach their ends.
All inputs are finite; a program needn't handle non-finite values.
Results may differ from the reference program's by a relative error of at most 0.013.
Values may be sent and summed in bfloat16 or wider, within the bound.
A program may use at most 64 MiB of HBM per device.

```python
import jax
import jax.numpy as jnp
from jax import lax

SAMP_DEV = 512
VARIANTS = 32768
BLOCK = 16
ITERS = 2
SAMPLES = 32768
N_SAMP = 64
N_VAR = 8


def frequency_table(key):
    spread = jax.random.uniform(key, (VARIANTS,), jnp.float32, jnp.log(0.05), jnp.log(0.5))
    return jnp.clip(jnp.exp(spread), 0.05, 0.5)


def draw_frequency(key, part):
    return frequency_table(key)


def draw_genotypes(key, part):
    centre = 2.0 * frequency_table(key)
    key = jax.random.fold_in(key, 7)
    factor = jax.random.uniform(key, (SAMPLES, VARIANTS), jnp.float32, 0.0, 2.0)
    return jnp.clip(centre * factor, 0.0, 2.0).astype(jnp.bfloat16)


def block_levels(stream_key, shape, shards, low, largest):
    def one(position, blocks):
        draws = jax.random.uniform(jax.random.fold_in(jax.random.fold_in(stream_key, 6), position), (blocks,), jnp.float32, low / len(shards), largest / len(shards))
        return jnp.repeat(jnp.exp(draws), shape[position] // blocks).reshape((-1,) + (1,) * (len(shape) - position - 1))

    factor_of = one(*shards[0])
    for cut in shards[1:]:
        factor_of = factor_of * one(*cut)
    return factor_of


def scatter_about(rng, dims, deviation, most, shards=(), kind=jnp.bfloat16):
    result = deviation * jax.random.normal(rng, dims, jnp.float32)
    if shards:
        result = result * block_levels(rng, dims, shards, -0.22, 0.18)
    return jnp.clip(result, -most, most).astype(kind)


def setup_inputs(seed: int = 0) -> dict:
    splits = jax.random.split(jax.random.key(seed), 4)
    return {
        "genotypes": draw_genotypes(jax.random.fold_in(splits[3], 71), 0),
        "frequency": draw_frequency(jax.random.fold_in(splits[3], 71), 0),
        "start_block": scatter_about(splits[2], (VARIANTS, BLOCK), 1.0, 6.0, ((0, 8),), jnp.float32),
    }


def standardize(rows, frequency):
    centre = 2.0 * frequency
    return ((rows.astype(jnp.float32) - centre) / jnp.sqrt(centre * (1.0 - frequency))).astype(jnp.bfloat16)

def rounded_sample_side(scaled, narrow):
    width = VARIANTS // N_VAR
    left = scaled.astype(jnp.float32).reshape(scaled.shape[0], N_VAR, width)
    right = narrow.astype(jnp.float32).reshape(N_VAR, width, BLOCK)
    partial_terms = jnp.einsum('svk,vkb->svb', left, right)
    rounded = lax.optimization_barrier(partial_terms.astype(jnp.bfloat16))
    return lax.optimization_barrier(jnp.sum(rounded.astype(jnp.float32), axis=1)).astype(jnp.bfloat16)

def one_pass(genotypes, frequency, basis_cols):
    blocks = genotypes.reshape(N_SAMP, SAMP_DEV, VARIANTS)
    narrow = basis_cols.astype(jnp.bfloat16)

    def step_rows(total, rows):
        scaled = standardize(rows, frequency)
        sample_block = rounded_sample_side(scaled, narrow)
        total = total + jnp.dot(scaled.T.astype(jnp.float32), sample_block.astype(jnp.float32), preferred_element_type=jnp.float32)
        return (total, 0)
    total, unused = lax.scan(step_rows, jnp.zeros((VARIANTS, BLOCK), jnp.float32), blocks)
    return total

def score_pass(genotypes, frequency, basis_cols):
    blocks = genotypes.reshape(N_SAMP, SAMP_DEV, VARIANTS)
    narrow = basis_cols.astype(jnp.bfloat16)

    def step_rows(carry, rows):
        scaled = standardize(rows, frequency)
        return (carry, jnp.dot(scaled.astype(jnp.float32), narrow.astype(jnp.float32), preferred_element_type=jnp.float32))
    unused, pieces = lax.scan(step_rows, jnp.float32(0.0), blocks)
    return pieces.reshape(SAMP_DEV * N_SAMP, BLOCK)

def reference(genotypes, frequency, start_block):
    basis_cols = start_block
    for iteration in range(ITERS):
        variant_block = one_pass(genotypes, frequency, basis_cols)
        gram_matrix = jnp.dot(variant_block.T, variant_block, precision=lax.Precision.HIGHEST)
        factor = jnp.linalg.cholesky(gram_matrix)
        basis_cols = jax.scipy.linalg.solve_triangular(factor, variant_block.T, lower=True).T
    scores = score_pass(genotypes, frequency, basis_cols)
    loadings = basis_cols * jnp.sqrt(jnp.float32(VARIANTS))
    return (loadings, scores)
```

```python
import functools

import jax
import jax.numpy as jnp
from jax import lax
from jax.experimental import pallas as pl
from jax.experimental.pallas import tpu as pltpu
from jax.sharding import PartitionSpec as P

MESH = pl.DeviceIdType.MESH
F32, BF16 = jnp.float32, jnp.bfloat16
BLOCK = 16
VARIANTS = 32768
ROWS, COLS = 512, 4096
N_VAR = 8
NEAR, FAR = 16, 4
PIECE = COLS // NEAR
LOADS = 4
FIRST_WIRE, SECOND_WIRE = F32, F32


def split(a, terms):
    parts, rest = [], a
    for _ in range(terms):
        part = rest.astype(BF16)
        parts.append(part)
        rest = rest - part.astype(F32)
    return parts


def nt(a, b, **kw):
    return lax.dot_general(a, b, (((1,), (1,)), ((), ())), preferred_element_type=F32, **kw)


def row_of(a, k):
    return jnp.broadcast_to(a[k : k + 1, :], a.shape)


def inverse_factor(gram):
    shape = (BLOCK, 128)
    row = lax.broadcasted_iota(jnp.int32, shape, 0)
    lane = lax.broadcasted_iota(jnp.int32, shape, 1)
    columns = [jnp.broadcast_to(gram[:, j : j + 1], shape) for j in range(BLOCK)]
    inverse = jnp.where(row == lane, 1.0, 0.0).astype(F32)
    roots = jnp.zeros(shape, F32)
    for k in range(BLOCK):
        column = columns[k]
        pivot = row_of(column, k)
        factor = jnp.where(row > k, column / pivot, 0.0)
        roots = jnp.where(row == k, 1.0 / jnp.sqrt(pivot), roots)
        for j in range(k + 1, BLOCK):
            columns[j] = columns[j] - factor * row_of(column, j)
        inverse = inverse - factor * row_of(inverse, k)
    return inverse * roots


def kernel(
    g_hbm, freq_ref, start_ref, load_ref, score_ref,
    g, terms, gram_terms, centre, scale,
    p_first, p_slots, gram_slots,
    part_1, near_1, far_1, whole_1,
    part_2, near_2, far_2, whole_2,
    load_sems, pair_send, pair_recv, gram_send, gram_recv,
    near_send, near_recv, far_send, far_recv, whole_send, whole_recv,
):
    samp, var = lax.axis_index("samp"), lax.axis_index("var")
    z, x = lax.div(samp, 4), lax.rem(samp, 4)
    z_far, z_near = lax.div(z, 4), lax.rem(z, 4)
    y, core = lax.div(var, 2), lax.rem(var, 2)
    my_near = z_near * 4 + x

    var_peers = []
    for dy in (2, 1, 3, 0):
        for dc in (0, 1):
            if dy or dc:
                other = lax.rem(y + dy, 4) * 2 + lax.rem(core + dc, 2)
                var_peers.append((other, (samp, other)))
    near_peers = []
    for dz in (2, 1, 3, 0):
        for dx in (2, 1, 3, 0):
            if dz or dx:
                slot = lax.rem(z_near + dz, 4) * 4 + lax.rem(x + dx, 4)
                near_peers.append((slot, (z_far * 16 + slot, var)))
    far_peers = []
    for d in (2, 1, 3):
        slot = lax.rem(z_far + d, 4)
        far_peers.append((slot, (slot * 16 + my_near, var)))

    loads = []
    step = ROWS // LOADS
    for i in range(LOADS):
        rows = pl.ds(i * step, step)
        loads.append(pltpu.make_async_copy(g_hbm.at[rows, :], g.at[rows, :], load_sems.at[i]))
        loads[-1].start()

    barrier = pltpu.get_barrier_semaphore()
    everyone = far_peers + near_peers + var_peers
    for _, device in everyone:
        pl.semaphore_signal(barrier, 1, device_id=device, device_id_type=MESH)

    def copies(peers, source, target, mine, send, recv):
        return [
            (
                slot,
                pltpu.make_async_remote_copy(
                    src_ref=source(slot), dst_ref=target.at[mine], send_sem=send.at[slot], recv_sem=recv.at[mine],
                    device_id=device, device_id_type=MESH,
                ),
                pltpu.make_async_remote_copy(
                    src_ref=source(slot), dst_ref=target.at[slot], send_sem=send.at[slot], recv_sem=recv.at[slot],
                    device_id=device, device_id_type=MESH,
                ),
            )
            for slot, device in peers
        ]

    sent = []

    def start(group):
        for _, out, _ in group:
            out.start()
        sent.extend(group)

    def wait(group):
        for _, _, back in group:
            back.wait_recv()

    centre[...] = 2.0 * freq_ref[...]
    scale[...] = 1.0 / jnp.sqrt(centre[...] * (1.0 - centre[...] * 0.5))

    def fill(block, columns):
        scaled = block * scale[:, columns]
        high, low = split(scaled, 2)
        terms[0:BLOCK, columns] = high
        terms[BLOCK : 2 * BLOCK, columns] = low
        return jnp.sum((high.astype(F32) + low.astype(F32)) * centre[:, columns], axis=1, keepdims=True)

    def sample_product(rows, shift):
        both = nt(terms[...], g[rows, :])
        return both[0:BLOCK] + both[BLOCK:] - shift

    def exchange_samples(index, slots):
        group = copies(var_peers, lambda slot: slots.at[var], slots, var, pair_send.at[index], pair_recv.at[index])
        start(group)
        return group

    def total_of(slots, n):
        total = slots[0].astype(F32)
        for i in range(1, n):
            total = total + slots[i].astype(F32)
        return total

    def exchange_gram(index, whole):
        for b in range(NEAR):
            parts = split(whole[b].astype(F32), 3)
            for t in range(3):
                gram_terms[t * BLOCK : (t + 1) * BLOCK, b * PIECE : (b + 1) * PIECE] = parts[t]
        products = nt(gram_terms[...], gram_terms[...])
        gram = jnp.zeros((BLOCK, BLOCK), F32)
        for a, b in ((2, 2), (2, 1), (1, 2), (2, 0), (0, 2), (1, 1), (1, 0), (0, 1), (0, 0)):
            gram = gram + products[a * BLOCK : (a + 1) * BLOCK, b * BLOCK : (b + 1) * BLOCK]
        slots = gram_slots.at[index]
        slots[var, :, 0:BLOCK] = gram
        slots[var, :, BLOCK:] = jnp.zeros((BLOCK, 128 - BLOCK), F32)
        group = copies(var_peers, lambda slot: slots.at[var], slots, var, gram_send.at[index], gram_recv.at[index])
        start(group)
        return group

    def variant_pass(index, sample_block, part, near, far, whole):
        narrow = sample_block.astype(BF16)
        shift = jnp.sum(narrow.astype(F32), axis=1, keepdims=True)
        for b in range(NEAR):
            columns = slice(b * PIECE, (b + 1) * PIECE)
            product = jnp.dot(narrow, g[:, columns], preferred_element_type=F32)
            part[b] = ((product - shift * centre[:, columns]) * scale[:, columns]).astype(part.dtype)
        group = copies(near_peers, lambda slot: part.at[slot], near, my_near, near_send.at[index], near_recv.at[index])
        start(group)
        total = part[my_near].astype(F32)
        for slot, _, back in reversed(group):
            back.wait_recv()
            total = total + near[slot].astype(F32)
        far[z_far] = total.astype(far.dtype)
        group = copies(far_peers, lambda slot: far.at[z_far], far, z_far, far_send.at[index], far_recv.at[index])
        start(group)
        wait(group)
        whole[my_near] = total_of(far, FAR).astype(whole.dtype)
        group = copies(near_peers, lambda slot: whole.at[my_near], whole, my_near, whole_send.at[index], whole_recv.at[index])
        start(group)
        wait(group)

    def sample_pass(index, whole):
        shift = jnp.zeros((BLOCK, 1), F32)
        for b in range(NEAR):
            shift = shift + fill(whole[b].astype(F32), slice(b * PIECE, (b + 1) * PIECE))
        slots = p_slots.at[index]
        slots[var] = sample_product(slice(None), shift)
        return exchange_samples(index + 1, slots)

    def whitener(index, group):
        wait(group)
        return inverse_factor(total_of(gram_slots.at[index], N_VAR)[:, 0:BLOCK])[:, 0:BLOCK]

    shift = fill(start_ref[...].astype(BF16).astype(F32), slice(None))
    for i in range(LOADS):
        loads[i].wait()
        rows = slice(i * step, (i + 1) * step)
        p_first[var, :, rows] = sample_product(rows, shift).astype(BF16)
    pl.semaphore_wait(barrier, len(everyone))
    group = exchange_samples(0, p_first)
    wait(group)
    variant_pass(0, total_of(p_first, N_VAR), part_1, near_1, far_1, whole_1)

    gram_group = exchange_gram(0, whole_1)
    group = sample_pass(0, whole_1)
    whiten = whitener(0, gram_group)
    wait(group)
    sample_block = jnp.dot(whiten, total_of(p_slots.at[0], N_VAR), precision=lax.Precision.HIGHEST, preferred_element_type=F32)
    variant_pass(1, sample_block, part_2, near_2, far_2, whole_2)

    gram_group = exchange_gram(1, whole_2)
    group = sample_pass(1, whole_2)
    whiten = whitener(1, gram_group)
    scaled = whiten * jnp.sqrt(jnp.float32(VARIANTS))
    for b in range(NEAR):
        load_ref[:, b * PIECE : (b + 1) * PIECE] = jnp.dot(
            scaled, whole_2[b].astype(F32), precision=lax.Precision.HIGHEST, preferred_element_type=F32
        )
    wait(group)
    score_ref[...] = jnp.dot(whiten, total_of(p_slots.at[1], N_VAR), precision=lax.Precision.HIGHEST, preferred_element_type=F32)
    for _, out, _ in sent:
        out.wait_send()


def local(genotypes, frequency, start_block):
    piece = (BLOCK, PIECE)
    scratch = [
        pltpu.VMEM((ROWS, COLS), BF16),
        pltpu.VMEM((2 * BLOCK, COLS), BF16),
        pltpu.VMEM((3 * BLOCK, COLS), BF16),
        pltpu.VMEM((1, COLS), F32),
        pltpu.VMEM((1, COLS), F32),
        pltpu.VMEM((N_VAR, BLOCK, ROWS), BF16),
        pltpu.VMEM((2, N_VAR, BLOCK, ROWS), F32),
        pltpu.VMEM((2, N_VAR, BLOCK, 128), F32),
    ]
    for wire in (FIRST_WIRE, SECOND_WIRE):
        scratch += [pltpu.VMEM((n,) + piece, wire) for n in (NEAR, NEAR, FAR, NEAR)]
    scratch += [pltpu.SemaphoreType.DMA((LOADS,))]
    for n in ((3, N_VAR), (2, N_VAR), (2, NEAR), (2, FAR), (2, NEAR)):
        scratch += [pltpu.SemaphoreType.DMA(n)] * 2
    vmem = pl.BlockSpec(memory_space=pltpu.VMEM)
    loadings, scores = pl.pallas_call(
        kernel,
        name="subspace",
        out_shape=(jax.ShapeDtypeStruct((BLOCK, COLS), F32), jax.ShapeDtypeStruct((BLOCK, ROWS), F32)),
        in_specs=[pl.BlockSpec(memory_space=pltpu.HBM), vmem, vmem],
        out_specs=(vmem, vmem),
        scratch_shapes=scratch,
        compiler_params=pltpu.CompilerParams(collective_id=0, has_side_effects=True, vmem_limit_bytes=48 << 20),
        cost_estimate=pl.CostEstimate(flops=5 * 2 * ROWS * COLS * BLOCK, bytes_accessed=2 * ROWS * COLS, transcendentals=0),
    )(genotypes, frequency.reshape(1, COLS), start_block.T)
    return loadings.T, scores.T


def solution(mesh):
    return jax.shard_map(
        local,
        mesh=mesh,
        in_specs=(P("samp", "var"), P("var"), P("var", None)),
        out_specs=(P("var", None), P("samp", None)),
        check_vma=False,
    )
```

```python
import jax
import jax.numpy as jnp
from jax import lax
from jax.experimental import pallas as pl
from jax.experimental.pallas import tpu as pltpu
from jax.sharding import PartitionSpec as P

MESH = pl.DeviceIdType.MESH
F32, BF16 = jnp.float32, jnp.bfloat16
BLOCK = 16
VARIANTS = 32768
ROWS, COLS = 512, 4096
N_VAR = 8
NEAR, FAR = 16, 4
PIECE = COLS // NEAR
LOADS = 8
FIRST_WIRE, SECOND_WIRE = F32, BF16


def split(a, terms):
    parts, rest = [], a
    for _ in range(terms):
        part = rest.astype(BF16)
        parts.append(part)
        rest = rest - part.astype(F32)
    return parts


def nt(a, b):
    return lax.dot_general(a, b, (((1,), (1,)), ((), ())), preferred_element_type=F32)


def full(a, b):
    return jnp.dot(a, b, precision=lax.Precision.HIGHEST, preferred_element_type=F32)


def row_of(a, k):
    return jnp.broadcast_to(a[k : k + 1, :], a.shape)


def inverse_factor(gram):
    shape = (BLOCK, 128)
    row = lax.broadcasted_iota(jnp.int32, shape, 0)
    lane = lax.broadcasted_iota(jnp.int32, shape, 1)
    columns = [jnp.broadcast_to(gram[:, j : j + 1], shape) for j in range(BLOCK)]
    inverse = jnp.where(row == lane, 1.0, 0.0).astype(F32)
    roots = jnp.zeros(shape, F32)
    for k in range(BLOCK):
        column = columns[k]
        pivot = row_of(column, k)
        factor = jnp.where(row > k, column / pivot, 0.0)
        roots = jnp.where(row == k, 1.0 / jnp.sqrt(pivot), roots)
        for j in range(k + 1, BLOCK):
            columns[j] = columns[j] - factor * row_of(column, j)
        inverse = inverse - factor * row_of(inverse, k)
    return inverse * roots


def kernel(
    g_hbm, freq_hbm, start_hbm, load_ref, score_ref,
    g, g_t, start_block, frequency, centre, scale,
    p_first, p_slots, gram_rows, gram_slots,
    part_1, near_1, far_1, whole_1,
    part_2, near_2, far_2, whole_2,
    load_sems, pair_send, pair_recv, gram_send, gram_recv,
    near_send, near_recv, far_send, far_recv, whole_send, whole_recv, opposite_sem, diagonal_sem,
):
    samp, var = lax.axis_index("samp"), lax.axis_index("var")
    z, x = lax.div(samp, 4), lax.rem(samp, 4)
    z_far, z_near = lax.div(z, 4), lax.rem(z, 4)
    y, core = lax.div(var, 2), lax.rem(var, 2)
    my_near = z_near * 4 + x

    var_peers = []
    for dy in (2, 1, 3, 0):
        for dc in (0, 1):
            if dy or dc:
                other = lax.rem(y + dy, 4) * 2 + lax.rem(core + dc, 2)
                var_peers.append((other, (samp, other)))
    near_peers = []
    for dz in (2, 1, 3, 0):
        for dx in (2, 1, 3, 0):
            if dz or dx:
                slot = lax.rem(z_near + dz, 4) * 4 + lax.rem(x + dx, 4)
                near_peers.append((slot, (z_far * 16 + slot, var)))
    far_peers = []
    for d in (2, 1, 3):
        slot = lax.rem(z_far + d, 4)
        far_peers.append((slot, (slot * 16 + my_near, var)))

    barrier = pltpu.get_barrier_semaphore()
    along_x = [near_peers[i] for i in (12, 13, 14)]
    along_z = [near_peers[i] for i in (3, 7, 11)]
    everyone = far_peers[1:] + along_z + along_x + var_peers
    for _, device in everyone:
        pl.semaphore_signal(barrier, 1, device_id=device, device_id_type=MESH)

    loads = [
        pltpu.make_async_copy(freq_hbm, frequency, load_sems.at[0]),
        pltpu.make_async_copy(start_hbm, start_block, load_sems.at[1]),
    ]
    step = COLS // LOADS
    for i in range(LOADS):
        columns = pl.ds(i * step, step)
        loads.append(pltpu.make_async_copy(g_hbm.at[:, columns], g.at[:, columns], load_sems.at[i + 2]))
    for load in loads:
        load.start()

    def copies(peers, source, target, mine, send, recv):
        return [
            (
                slot,
                pltpu.make_async_remote_copy(
                    src_ref=source(slot), dst_ref=target.at[mine], send_sem=send.at[slot], recv_sem=recv.at[mine],
                    device_id=device, device_id_type=MESH,
                ),
                pltpu.make_async_remote_copy(
                    src_ref=source(slot), dst_ref=target.at[slot], send_sem=send.at[slot], recv_sem=recv.at[slot],
                    device_id=device, device_id_type=MESH,
                ),
            )
            for slot, device in peers
        ]

    sent = []

    def start(group):
        for _, out, _ in group:
            out.start()
        sent.extend(group)

    def wait(group):
        for _, _, back in group:
            back.wait_recv()

    def scaled_terms(block, b):
        high, low = split(block * scale[b], 2)
        return jnp.concatenate([high, low], axis=0), (high.astype(F32) + low.astype(F32)) * centre[b]

    def sample_product(total, shift):
        return total[0:BLOCK] + total[BLOCK:] - jnp.sum(shift, axis=1, keepdims=True)

    def exchange_samples(index, slots):
        group = copies(var_peers, lambda slot: slots.at[var], slots, var, pair_send.at[index], pair_recv.at[index])
        start(group)
        return group

    def total_of(slots, n):
        total = slots[0].astype(F32)
        for i in range(1, n):
            total = total + slots[i].astype(F32)
        return total

    def variant_pass(index, sample_block, part, near, far, whole):
        narrow = sample_block.astype(BF16)
        shift = jnp.sum(narrow.astype(F32), axis=1, keepdims=True)
        for b in range(NEAR):
            product = jnp.dot(narrow, g[:, b * PIECE : (b + 1) * PIECE], preferred_element_type=F32)
            part[b] = ((product - shift * centre[b]) * scale[b]).astype(part.dtype)
        if index == 0:
            pl.semaphore_wait(diagonal_sem, len(along_x))
        group = copies(near_peers, lambda slot: part.at[slot], near, my_near, near_send.at[index], near_recv.at[index])
        start(group)
        total = part[my_near].astype(F32)
        for slot, _, back in reversed(group):
            back.wait_recv()
            total = total + near[slot].astype(F32)
        far[z_far] = total.astype(far.dtype)
        if index == 0:
            pl.semaphore_wait(opposite_sem, 1)
        group = copies(far_peers, lambda slot: far.at[z_far], far, z_far, far_send.at[index], far_recv.at[index])
        start(group)
        wait(group)
        whole[my_near] = total_of(far, FAR).astype(whole.dtype)
        group = copies(near_peers, lambda slot: whole.at[my_near], whole, my_near, whole_send.at[index], whole_recv.at[index])
        start(group)
        return group

    def sample_pass(index, whole, arriving):
        exact = whole.dtype == BF16
        total, shift = jnp.zeros((2 * BLOCK, ROWS), F32), jnp.zeros((BLOCK, PIECE), F32)
        for dz in (0, 1, 3, 2):
            z_row = lax.rem(z_near + dz, 4)
            first = 4 * (2, 1, 3, 0).index(dz)
            wait(arriving[first : first + 4])
            blocks = [whole[z_row * 4 + i].astype(F32) for i in range(4)]
            gram = jnp.zeros((BLOCK, BLOCK), F32)
            for block in blocks:
                if exact:
                    terms = block.astype(BF16)
                    gram = gram + nt(terms, terms)
                else:
                    high, middle, low = split(block, 3)
                    gram = gram + nt(
                        jnp.concatenate([high, high, middle, high, low, middle], axis=1),
                        jnp.concatenate([high, middle, high, low, high, middle], axis=1),
                    )
            gram_rows[z_row, :, 0:BLOCK] = gram
            rows = []
            for i, block in enumerate(blocks):
                terms, shifted = scaled_terms(block, z_row * 4 + i)
                rows.append(terms)
                shift = shift + shifted
            depth = 4 * PIECE
            total = total + jnp.dot(
                jnp.concatenate(rows, axis=1),
                g_t[pl.ds(pl.multiple_of(z_row * depth, depth), depth), :],
                preferred_element_type=F32,
            )
        gram = gram_rows[0, :, 0:BLOCK]
        for i in range(1, 4):
            gram = gram + gram_rows[i, :, 0:BLOCK]
        whole_gram = gram_slots.at[index]
        whole_gram[var, :, 0:BLOCK] = gram
        whole_gram[var, :, BLOCK:] = jnp.zeros((BLOCK, 128 - BLOCK), F32)
        gram_group = copies(
            var_peers, lambda slot: whole_gram.at[var], whole_gram, var, gram_send.at[index], gram_recv.at[index]
        )
        start(gram_group)
        slots = p_slots.at[index]
        slots[var] = sample_product(total, shift)
        group = exchange_samples(index + 1, slots)
        wait(gram_group)
        return group, inverse_factor(total_of(whole_gram, N_VAR)[:, 0:BLOCK])[:, 0:BLOCK]

    loads[0].wait()
    centre[...] = 2.0 * frequency[...]
    scale[...] = 1.0 / jnp.sqrt(centre[...] * (1.0 - frequency[...]))
    loads[1].wait()
    total, shift = jnp.zeros((2 * BLOCK, ROWS), F32), jnp.zeros((BLOCK, PIECE), F32)
    for i in range(LOADS):
        loads[i + 2].wait()
        for b in range(i * NEAR // LOADS, (i + 1) * NEAR // LOADS):
            columns = slice(b * PIECE, (b + 1) * PIECE)
            terms, shifted = scaled_terms(start_block[:, columns].astype(BF16).astype(F32), b)
            total = total + nt(terms, g[:, columns])
            shift = shift + shifted
    p_first[var] = sample_product(total, shift).astype(BF16)
    pl.semaphore_wait(barrier, len(everyone))
    pl.semaphore_signal(opposite_sem, 1, device_id=far_peers[1][1], device_id_type=MESH)
    for _, device in along_x:
        pl.semaphore_signal(diagonal_sem, 1, device_id=device, device_id_type=MESH)
    group = exchange_samples(0, p_first)
    for b in range(NEAR):
        g_t[b * PIECE : (b + 1) * PIECE, :] = g[:, b * PIECE : (b + 1) * PIECE].T
    wait(group)
    arriving = variant_pass(0, total_of(p_first, N_VAR), part_1, near_1, far_1, whole_1)

    group, whiten = sample_pass(0, whole_1, arriving)
    wait(group)
    sample_block = full(whiten, total_of(p_slots.at[0], N_VAR))
    arriving = variant_pass(1, sample_block, part_2, near_2, far_2, whole_2)

    group, whiten = sample_pass(1, whole_2, arriving)
    scaled = whiten * jnp.sqrt(jnp.float32(VARIANTS))
    for b in range(NEAR):
        load_ref[:, b * PIECE : (b + 1) * PIECE] = full(scaled, whole_2[b].astype(F32))
    wait(group)
    score_ref[...] = full(whiten, total_of(p_slots.at[1], N_VAR))
    for _, out, _ in sent:
        out.wait_send()


def local(genotypes, frequency, start_block):
    piece = (BLOCK, PIECE)
    row = (NEAR, 1, PIECE)
    scratch = [
        pltpu.VMEM((ROWS, COLS), BF16),
        pltpu.VMEM((COLS, ROWS), BF16),
        pltpu.VMEM((BLOCK, COLS), F32),
        pltpu.VMEM(row, F32),
        pltpu.VMEM(row, F32),
        pltpu.VMEM(row, F32),
        pltpu.VMEM((N_VAR, BLOCK, ROWS), BF16),
        pltpu.VMEM((2, N_VAR, BLOCK, ROWS), F32),
        pltpu.VMEM((4, BLOCK, 128), F32),
        pltpu.VMEM((2, N_VAR, BLOCK, 128), F32),
    ]
    for wire in (FIRST_WIRE, SECOND_WIRE):
        scratch += [pltpu.VMEM((n,) + piece, wire) for n in (NEAR, NEAR, FAR, NEAR)]
    scratch += [pltpu.SemaphoreType.DMA((LOADS + 2,))]
    for n in ((3, N_VAR), (2, N_VAR), (2, NEAR), (2, FAR), (2, NEAR)):
        scratch += [pltpu.SemaphoreType.DMA(n)] * 2
    scratch += [pltpu.SemaphoreType.REGULAR] * 2
    vmem, hbm = pl.BlockSpec(memory_space=pltpu.VMEM), pl.BlockSpec(memory_space=pl.ANY)
    loadings, scores = pl.pallas_call(
        kernel,
        name="subspace",
        out_shape=(pltpu.VMEM((BLOCK, COLS), F32), pltpu.VMEM((BLOCK, ROWS), F32)),
        in_specs=[hbm, hbm, hbm],
        out_specs=(vmem, vmem),
        scratch_shapes=scratch,
        compiler_params=pltpu.CompilerParams(collective_id=0, has_side_effects=True, vmem_limit_bytes=48 << 20),
        cost_estimate=pl.CostEstimate(flops=5 * 2 * ROWS * COLS * BLOCK, bytes_accessed=2 * ROWS * COLS, transcendentals=0),
    )(*(pltpu.with_memory_space_constraint(a, pltpu.HBM) for a in (genotypes, frequency.reshape(row), start_block.T)))
    return loadings.T, scores.T


def solution(mesh):
    return jax.shard_map(
        local,
        mesh=mesh,
        in_specs=(P("samp", "var"), P("var"), P("var", None)),
        out_specs=(P("var", None), P("samp", None)),
        check_vma=False,
    )
```

```python
import jax
import jax.numpy as jnp
from jax import lax
from jax.experimental import pallas as pl
from jax.experimental.pallas import tpu as pltpu
from jax.sharding import PartitionSpec as P

MESH = pl.DeviceIdType.MESH
F32, BF16 = jnp.float32, jnp.bfloat16
BLOCK = 16
VARIANTS = 32768
ROWS, COLS = 512, 4096
N_VAR = 8
NEAR, FAR = 16, 4
PARTS = 2
PIECE = COLS // NEAR // PARTS
LOADS = 8


def split(a, terms):
    parts, rest = [], a
    for _ in range(terms):
        part = rest.astype(BF16)
        parts.append(part)
        rest = rest - part.astype(F32)
    return parts


def nt(a, b):
    return lax.dot_general(a, b, (((1,), (1,)), ((), ())), preferred_element_type=F32)


def full(a, b):
    return jnp.dot(a, b, precision=lax.Precision.HIGHEST, preferred_element_type=F32)


def row_of(a, k):
    return jnp.broadcast_to(a[k : k + 1, :], a.shape)


def inverse_factor(gram):
    shape = (BLOCK, 128)
    row = lax.broadcasted_iota(jnp.int32, shape, 0)
    lane = lax.broadcasted_iota(jnp.int32, shape, 1)
    columns = [jnp.broadcast_to(gram[:, j : j + 1], shape) for j in range(BLOCK)]
    inverse = jnp.where(row == lane, 1.0, 0.0).astype(F32)
    roots = jnp.zeros(shape, F32)
    for k in range(BLOCK):
        column = columns[k]
        pivot = row_of(column, k)
        factor = jnp.where(row > k, column / pivot, 0.0)
        roots = jnp.where(row == k, 1.0 / jnp.sqrt(pivot), roots)
        for j in range(k + 1, BLOCK):
            columns[j] = columns[j] - factor * row_of(column, j)
        inverse = inverse - factor * row_of(inverse, k)
    return inverse * roots


def kernel(
    g_hbm, freq_hbm, start_hbm, load_ref, score_ref,
    g, g_t, start_block, frequency, centre, scale,
    p_first, p_slots, gram_rows, gram_slots,
    part, near, far, whole,
    load_sems, pair_send, pair_recv, gram_send, gram_recv,
    near_send, near_recv, far_send, far_recv, whole_send, whole_recv, opposite_sem, diagonal_sem,
):
    samp, var = lax.axis_index("samp"), lax.axis_index("var")
    z, x = lax.div(samp, 4), lax.rem(samp, 4)
    z_far, z_near = lax.div(z, 4), lax.rem(z, 4)
    y, core = lax.div(var, 2), lax.rem(var, 2)
    my_near = z_near * 4 + x

    var_peers = []
    for dy in (2, 1, 3, 0):
        for dc in (0, 1):
            if dy or dc:
                other = lax.rem(y + dy, 4) * 2 + lax.rem(core + dc, 2)
                var_peers.append((other, (samp, other)))
    z_at = [z_near, z_near + 1 - 2 * lax.rem(z_near, 2), lax.rem(z_near + 2, 4), 3 - z_near]
    steps = [(a, b) for a in range(4) for b in range(4) if a or b]
    steps.sort(key=lambda step: -step[0] - (0, 1, 2, 1.6)[step[1]])
    near_peers = []
    for a, b in steps:
        slot = z_at[a] * 4 + lax.rem(x + b, 4)
        near_peers.append((slot, (z_far * 16 + slot, var)))
    far_peers = []
    for d in (2, 1, 3):
        slot = lax.rem(z_far + d, 4)
        far_peers.append((slot, (slot * 16 + my_near, var)))

    barrier = pltpu.get_barrier_semaphore()
    along_x = [near_peers[i] for i, (a, b) in enumerate(steps) if a == 0]
    along_z = [near_peers[i] for i, (a, b) in enumerate(steps) if b == 0]
    everyone = far_peers[1:] + along_z + along_x + var_peers
    for _, device in everyone:
        pl.semaphore_signal(barrier, 1, device_id=device, device_id_type=MESH)

    loads = [
        pltpu.make_async_copy(freq_hbm, frequency, load_sems.at[0]),
        pltpu.make_async_copy(start_hbm, start_block, load_sems.at[1]),
    ]
    step = COLS // LOADS
    for i in range(LOADS):
        columns = pl.ds(i * step, step)
        loads.append(pltpu.make_async_copy(g_hbm.at[:, columns], g.at[:, columns], load_sems.at[i + 2]))
    for load in loads:
        load.start()

    def copies(peers, source, target, mine, send, recv):
        return [
            (
                slot,
                pltpu.make_async_remote_copy(
                    src_ref=source(slot), dst_ref=target.at[mine], send_sem=send.at[slot], recv_sem=recv.at[mine],
                    device_id=device, device_id_type=MESH,
                ),
                pltpu.make_async_remote_copy(
                    src_ref=source(slot), dst_ref=target.at[slot], send_sem=send.at[slot], recv_sem=recv.at[slot],
                    device_id=device, device_id_type=MESH,
                ),
            )
            for slot, device in peers
        ]

    sent = []

    def start(group):
        for _, out, _ in group:
            out.start()
        sent.extend(group)

    def wait(group):
        for _, _, back in group:
            back.wait_recv()

    def scaled_terms(block, b):
        high, low = split(block * scale[b], 2)
        return jnp.concatenate([high, low], axis=0), (high.astype(F32) + low.astype(F32)) * centre[b]

    def sample_product(total, shift):
        return total[0:BLOCK] + total[BLOCK:] - jnp.sum(shift, axis=1, keepdims=True)

    def exchange_samples(index, slots):
        group = copies(var_peers, lambda slot: slots.at[var], slots, var, pair_send.at[index], pair_recv.at[index])
        start(group)
        return group

    def total_of(slots, n):
        total = slots[0].astype(F32)
        for i in range(1, n):
            total = total + slots[i].astype(F32)
        return total

    def variant_pass(index, sample_block):
        narrow = sample_block.astype(BF16)
        shift = jnp.sum(narrow.astype(F32), axis=1, keepdims=True)
        stages = [index * PARTS + h for h in range(PARTS)]
        groups = []
        for h, stage in enumerate(stages):
            for b in range(0, NEAR, 2):
                first = h * NEAR + b
                product = jnp.dot(narrow, g[:, first * PIECE : (first + 2) * PIECE], preferred_element_type=F32)
                for i in range(2):
                    piece = product[:, i * PIECE : (i + 1) * PIECE]
                    part[stage, b + i] = (piece - shift * centre[first + i]) * scale[first + i]
            if stage == 0:
                pl.semaphore_wait(diagonal_sem, len(along_x))
            group = copies(
                near_peers, lambda slot: part.at[stage, slot], near.at[stage], my_near, near_send.at[stage], near_recv.at[stage]
            )
            start(group)
            groups.append(group)
        far_groups = []
        for stage, group in zip(stages, groups):
            total = part[stage, my_near]
            for slot, _, back in reversed(group):
                back.wait_recv()
                total = total + near[stage, slot]
            far[stage, z_far] = total
            if stage == 0:
                pl.semaphore_wait(opposite_sem, 1)
            group = copies(
                far_peers, lambda slot: far.at[stage, z_far], far.at[stage], z_far, far_send.at[stage], far_recv.at[stage]
            )
            start(group)
            far_groups.append(group)
        groups = []
        for stage, group in zip(stages, far_groups):
            wait(group)
            whole[stage, my_near] = total_of(far.at[stage], FAR)
            group = copies(
                near_peers, lambda slot: whole.at[stage, my_near], whole.at[stage], my_near,
                whole_send.at[stage], whole_recv.at[stage],
            )
            start(group)
            groups.append(group)
        return groups

    def sample_pass(index, arriving):
        total, shift = jnp.zeros((2 * BLOCK, ROWS), F32), jnp.zeros((BLOCK, PIECE), F32)
        depth = 4 * PIECE
        for h in range(PARTS):
            for a in range(4):
                wait([arriving[h][i] for i, step in enumerate(steps) if step[0] == a])
                blocks = [whole[index * PARTS + h, z_at[a] * 4 + i] for i in range(4)]
                high, middle, low = split(jnp.concatenate(blocks, axis=1), 3)
                gram_rows[h * 4 + z_at[a], :, 0:BLOCK] = nt(
                    jnp.concatenate([high, high, middle, high, low, middle], axis=1),
                    jnp.concatenate([high, middle, high, low, high, middle], axis=1),
                )
                rows = []
                for i, block in enumerate(blocks):
                    terms, shifted = scaled_terms(block, h * NEAR + z_at[a] * 4 + i)
                    rows.append(terms)
                    shift = shift + shifted
                total = total + jnp.dot(
                    jnp.concatenate(rows, axis=1),
                    g_t[pl.ds(pl.multiple_of((h * 4 + z_at[a]) * depth, depth), depth), :],
                    preferred_element_type=F32,
                )
        whole_gram = gram_slots.at[index]
        whole_gram[var, :, 0:BLOCK] = sum((gram_rows[i, :, 0:BLOCK] for i in range(1, 4 * PARTS)), gram_rows[0, :, 0:BLOCK])
        whole_gram[var, :, BLOCK:] = jnp.zeros((BLOCK, 128 - BLOCK), F32)
        gram_group = copies(
            var_peers, lambda slot: whole_gram.at[var], whole_gram, var, gram_send.at[index], gram_recv.at[index]
        )
        start(gram_group)
        slots = p_slots.at[index]
        slots[var] = sample_product(total, shift)
        group = exchange_samples(index + 1, slots)
        wait(gram_group)
        return group, inverse_factor(total_of(whole_gram, N_VAR)[:, 0:BLOCK])[:, 0:BLOCK]

    loads[0].wait()
    centre[...] = 2.0 * frequency[...]
    scale[...] = 1.0 / jnp.sqrt(centre[...] * (1.0 - frequency[...]))
    loads[1].wait()
    total, shift = jnp.zeros((2 * BLOCK, ROWS), F32), jnp.zeros((BLOCK, PIECE), F32)
    for i in range(LOADS):
        loads[i + 2].wait()
        rows = []
        for b in range(i * step // PIECE, (i + 1) * step // PIECE):
            columns = slice(b * PIECE, (b + 1) * PIECE)
            terms, shifted = scaled_terms(start_block[:, columns].astype(BF16).astype(F32), b)
            rows.append(terms)
            shift = shift + shifted
        total = total + nt(jnp.concatenate(rows, axis=1), g[:, i * step : (i + 1) * step])
    p_first[var] = sample_product(total, shift).astype(BF16)
    pl.semaphore_wait(barrier, len(everyone))
    pl.semaphore_signal(opposite_sem, 1, device_id=far_peers[1][1], device_id_type=MESH)
    for _, device in along_x:
        pl.semaphore_signal(diagonal_sem, 1, device_id=device, device_id_type=MESH)
    group = exchange_samples(0, p_first)
    for i in range(LOADS):
        g_t[i * step : (i + 1) * step, :] = g[:, i * step : (i + 1) * step].T
    wait(group)
    arriving = variant_pass(0, total_of(p_first, N_VAR))

    group, whiten = sample_pass(0, arriving)
    wait(group)
    sample_block = full(whiten, total_of(p_slots.at[0], N_VAR))
    arriving = variant_pass(1, sample_block)

    group, whiten = sample_pass(1, arriving)
    scaled = whiten * jnp.sqrt(jnp.float32(VARIANTS))
    for b in range(0, PARTS * NEAR, 4):
        blocks = [whole[PARTS + b // NEAR, b % NEAR + i] for i in range(4)]
        load_ref[:, b * PIECE : (b + 4) * PIECE] = full(scaled, jnp.concatenate(blocks, axis=1))
    wait(group)
    score_ref[...] = full(whiten, total_of(p_slots.at[1], N_VAR))
    for _, out, _ in sent:
        out.wait_send()


def local(genotypes, frequency, start_block):
    piece = (BLOCK, PIECE)
    row = (PARTS * NEAR, 1, PIECE)
    scratch = [
        pltpu.VMEM((ROWS, COLS), BF16),
        pltpu.VMEM((COLS, ROWS), BF16),
        pltpu.VMEM((BLOCK, COLS), F32),
        pltpu.VMEM(row, F32),
        pltpu.VMEM(row, F32),
        pltpu.VMEM(row, F32),
        pltpu.VMEM((N_VAR, BLOCK, ROWS), BF16),
        pltpu.VMEM((2, N_VAR, BLOCK, ROWS), F32),
        pltpu.VMEM((4 * PARTS, BLOCK, 128), F32),
        pltpu.VMEM((2, N_VAR, BLOCK, 128), F32),
    ]
    stages = 2 * PARTS
    scratch += [pltpu.VMEM((stages, n) + piece, F32) for n in (NEAR, NEAR, FAR, NEAR)]
    scratch += [pltpu.SemaphoreType.DMA((LOADS + 2,))]
    for n in ((3, N_VAR), (2, N_VAR), (stages, NEAR), (stages, FAR), (stages, NEAR)):
        scratch += [pltpu.SemaphoreType.DMA(n)] * 2
    scratch += [pltpu.SemaphoreType.REGULAR] * 2
    vmem, hbm = pl.BlockSpec(memory_space=pltpu.VMEM), pl.BlockSpec(memory_space=pl.ANY)
    loadings, scores = pl.pallas_call(
        kernel,
        name="subspace",
        out_shape=(pltpu.VMEM((BLOCK, COLS), F32), pltpu.VMEM((BLOCK, ROWS), F32)),
        in_specs=[hbm, hbm, hbm],
        out_specs=(vmem, vmem),
        scratch_shapes=scratch,
        compiler_params=pltpu.CompilerParams(collective_id=0, has_side_effects=True, vmem_limit_bytes=48 << 20),
        cost_estimate=pl.CostEstimate(flops=5 * 2 * ROWS * COLS * BLOCK, bytes_accessed=2 * ROWS * COLS, transcendentals=0),
    )(*(pltpu.with_memory_space_constraint(a, pltpu.HBM) for a in (genotypes, frequency.reshape(row), start_block.T)))
    return loadings.T, scores.T


def solution(mesh):
    return jax.shard_map(
        local,
        mesh=mesh,
        in_specs=(P("samp", "var"), P("var"), P("var", None)),
        out_specs=(P("var", None), P("samp", None)),
        check_vma=False,
    )
```

```python
import jax
import jax.numpy as jnp
from jax import lax
from jax.experimental import pallas as pl
from jax.experimental.pallas import tpu as pltpu
from jax.sharding import PartitionSpec as P

MESH = pl.DeviceIdType.MESH
F32, BF16 = jnp.float32, jnp.bfloat16
BLOCK = 16
VARIANTS = 32768
ROWS, COLS = 512, 4096
N_VAR = 8
NEAR, FAR = 16, 4
PARTS = (2, 1)
WIRE = (F32, BF16)
UNIT = 128
LOADS = 8


def split(a, terms):
    parts, rest = [], a
    for _ in range(terms):
        part = rest.astype(BF16)
        parts.append(part)
        rest = rest - part.astype(F32)
    return parts


def nt(a, b):
    return lax.dot_general(a, b, (((1,), (1,)), ((), ())), preferred_element_type=F32)


def full(a, b):
    return jnp.dot(a, b, precision=lax.Precision.HIGHEST, preferred_element_type=F32)


def row_of(a, k):
    return jnp.broadcast_to(a[k : k + 1, :], a.shape)


def spread(matrix):
    shape = (BLOCK, 128)
    columns = [jnp.broadcast_to(matrix[:, j : j + 1], shape) for j in range(BLOCK)]
    return columns, lax.broadcasted_iota(jnp.int32, shape, 0), lax.broadcasted_iota(jnp.int32, shape, 1)


def factorise(gram):
    columns, row, lane = spread(gram)
    inverse = jnp.where(row == lane, 1.0, 0.0).astype(F32)
    roots, lower = jnp.zeros_like(inverse), jnp.zeros_like(inverse)
    for k in range(BLOCK):
        column = columns[k]
        pivot = row_of(column, k)
        root = 1.0 / jnp.sqrt(pivot)
        factor = jnp.where(row > k, column / pivot, 0.0)
        roots = jnp.where(row == k, root, roots)
        lower = jnp.where((lane == k) & (row >= k), column * root, lower)
        for j in range(k + 1, BLOCK):
            columns[j] = columns[j] - factor * row_of(column, j)
        inverse = inverse - factor * row_of(inverse, k)
    return lower, inverse * roots


def decorrelated(expected, rows):
    columns, row, _ = spread(expected)
    for k in range(BLOCK - 1):
        column = columns[k]
        factor = jnp.where(row > k, column / row_of(column, k), 0.0)
        factor = jnp.where(jnp.abs(factor) <= 8.0, factor, 0.0)
        for j in range(k + 1, BLOCK):
            columns[j] = columns[j] - factor * row_of(column, j)
        rows = rows - factor * row_of(rows, k)
    return rows


def kernel(
    g_hbm, freq_hbm, start_hbm, load_ref, score_ref,
    g, g_t, start_block, frequency, centre, scale,
    p_narrow, p_wide, gram_rows, gram_slots, start_inverse,
    part_1, near_1, far_1, whole_1,
    part_2, near_2, far_2, whole_2,
    load_sems, pair_send, pair_recv, gram_send, gram_recv,
    near_send, near_recv, far_send, far_recv, whole_send, whole_recv, opposite_sem, diagonal_sem,
):
    samp, var = lax.axis_index("samp"), lax.axis_index("var")
    z, x = lax.div(samp, 4), lax.rem(samp, 4)
    z_far, z_near = lax.div(z, 4), lax.rem(z, 4)
    y, core = lax.div(var, 2), lax.rem(var, 2)
    my_near = z_near * 4 + x

    var_peers = []
    for dy in (2, 1, 3, 0):
        for dc in (0, 1):
            if dy or dc:
                other = lax.rem(y + dy, 4) * 2 + lax.rem(core + dc, 2)
                var_peers.append((other, (samp, other)))
    z_at = [z_near, z_near + 1 - 2 * lax.rem(z_near, 2), lax.rem(z_near + 2, 4), 3 - z_near]
    steps = [(a, b) for a in range(4) for b in range(4) if a or b]
    steps.sort(key=lambda step: -step[0] - (0, 1, 2, 1.6)[step[1]])
    near_peers = []
    for a, b in steps:
        slot = z_at[a] * 4 + lax.rem(x + b, 4)
        near_peers.append((slot, (z_far * 16 + slot, var)))
    far_peers = []
    for d in (2, 1, 3):
        slot = lax.rem(z_far + d, 4)
        far_peers.append((slot, (slot * 16 + my_near, var)))

    barrier = pltpu.get_barrier_semaphore()
    along_x = [near_peers[i] for i, (a, b) in enumerate(steps) if a == 0]
    along_z = [near_peers[i] for i, (a, b) in enumerate(steps) if b == 0]
    everyone = far_peers[1:] + along_z + along_x + var_peers
    for _, device in everyone:
        pl.semaphore_signal(barrier, 1, device_id=device, device_id_type=MESH)

    loads = [
        pltpu.make_async_copy(freq_hbm, frequency, load_sems.at[0]),
        pltpu.make_async_copy(start_hbm, start_block, load_sems.at[1]),
    ]
    step = COLS // LOADS
    for i in range(LOADS):
        columns = pl.ds(i * step, step)
        loads.append(pltpu.make_async_copy(g_hbm.at[:, columns], g.at[:, columns], load_sems.at[i + 2]))
    for load in loads:
        load.start()

    def copies(peers, source, target, mine, send, recv):
        return [
            (
                slot,
                pltpu.make_async_remote_copy(
                    src_ref=source(slot), dst_ref=target.at[mine], send_sem=send.at[slot], recv_sem=recv.at[mine],
                    device_id=device, device_id_type=MESH,
                ),
                pltpu.make_async_remote_copy(
                    src_ref=source(slot), dst_ref=target.at[slot], send_sem=send.at[slot], recv_sem=recv.at[slot],
                    device_id=device, device_id_type=MESH,
                ),
            )
            for slot, device in peers
        ]

    sent = []

    def start(group):
        for _, out, _ in group:
            out.start()
        sent.extend(group)

    def wait(group):
        for _, _, back in group:
            back.wait_recv()

    def units(ref, first, n):
        return jnp.concatenate([ref[first + i] for i in range(n)], axis=1)

    def scaled_terms(block, first):
        n = block.shape[1] // UNIT
        high, low = split(block * units(scale, first, n), 2)
        exact = (high.astype(F32) + low.astype(F32)) * units(centre, first, n)
        return jnp.concatenate([high, low], axis=0), jnp.sum(exact, axis=1, keepdims=True)

    def sample_product(total, shift):
        return total[0:BLOCK] + total[BLOCK:] - shift

    def exchange(slots, send, recv):
        group = copies(var_peers, lambda slot: slots.at[var], slots, var, send, recv)
        start(group)
        return group

    def exchange_gram(index, gram):
        slots = gram_slots.at[index]
        slots[var, :, 0:BLOCK] = gram
        slots[var, :, BLOCK:] = jnp.zeros((BLOCK, 128 - BLOCK), F32)
        return exchange(slots, gram_send.at[index], gram_recv.at[index])

    def gram_of(index, group):
        wait(group)
        return total_of(gram_slots.at[index], N_VAR)[:, 0:BLOCK]

    def total_of(slots, n):
        total = slots[0].astype(F32)
        for i in range(1, n):
            total = total + slots[i].astype(F32)
        return total

    blocks = ((part_1, near_1, far_1, whole_1), (part_2, near_2, far_2, whole_2))
    first_stage = (0, PARTS[0])

    def variant_pass(index, sample_block, meanwhile):
        part, near, far, whole = blocks[index]
        wire = part.dtype
        piece = part.shape[-1]
        chunk = max(piece, 2 * UNIT)
        narrow = sample_block.astype(BF16)
        shift = jnp.sum(narrow.astype(F32), axis=1, keepdims=True)
        groups = []
        for h in range(PARTS[index]):
            stage = first_stage[index] + h
            for b in range(0, NEAR * piece, chunk):
                first = h * NEAR * piece + b
                product = jnp.dot(narrow, g[:, first : first + chunk], preferred_element_type=F32)
                n = chunk // UNIT
                product = (product - shift * units(centre, first // UNIT, n)) * units(scale, first // UNIT, n)
                for i in range(chunk // piece):
                    part[h, b // piece + i] = product[:, i * piece : (i + 1) * piece].astype(wire)
            if stage == 0:
                pl.semaphore_wait(diagonal_sem, len(along_x))
            group = copies(
                near_peers, lambda slot: part.at[h, slot], near.at[h], my_near, near_send.at[stage], near_recv.at[stage]
            )
            start(group)
            groups.append(group)
        meanwhile()
        far_groups = []
        for h, group in enumerate(groups):
            stage = first_stage[index] + h
            total = part[h, my_near].astype(F32)
            for slot, _, back in reversed(group):
                back.wait_recv()
                total = total + near[h, slot].astype(F32)
            far[h, z_far] = total.astype(wire)
            if stage == 0:
                pl.semaphore_wait(opposite_sem, 1)
            group = copies(far_peers, lambda slot: far.at[h, z_far], far.at[h], z_far, far_send.at[stage], far_recv.at[stage])
            start(group)
            far_groups.append(group)
        groups = []
        for h, group in enumerate(far_groups):
            stage = first_stage[index] + h
            wait(group)
            whole[h, my_near] = total_of(far.at[h], FAR).astype(wire)
            group = copies(
                near_peers, lambda slot: whole.at[h, my_near], whole.at[h], my_near, whole_send.at[stage], whole_recv.at[stage]
            )
            start(group)
            groups.append(group)
        return groups

    def sample_pass(index, arriving, slots, send, recv):
        whole = blocks[index][-1]
        depth = 4 * whole.shape[-1]
        total, shift = jnp.zeros((2 * BLOCK, ROWS), F32), jnp.zeros((BLOCK, 1), F32)
        for h in range(PARTS[index]):
            for a in range(4):
                wait([arriving[h][i] for i, step in enumerate(steps) if step[0] == a])
                block = jnp.concatenate([whole[h, z_at[a] * 4 + i] for i in range(4)], axis=1)
                if whole.dtype == BF16:
                    left = right = block
                else:
                    high, middle, low = split(block, 3)
                    left = jnp.concatenate([high, high, middle, high, low, middle], axis=1)
                    right = jnp.concatenate([high, middle, high, low, high, middle], axis=1)
                place = h * 4 + z_at[a]
                gram_rows[place, :, 0:BLOCK] = nt(left, right)
                terms, shifted = scaled_terms(block.astype(F32), place * (depth // UNIT))
                shift = shift + shifted
                total = total + jnp.dot(
                    terms, g_t[pl.ds(pl.multiple_of(place * depth, depth), depth), :], preferred_element_type=F32
                )
        gram = gram_rows[0, :, 0:BLOCK]
        for i in range(1, 4 * PARTS[index]):
            gram = gram + gram_rows[i, :, 0:BLOCK]
        gram_group = exchange_gram(index + 1, gram)
        slots[var] = sample_product(total, shift).astype(slots.dtype)
        return exchange(slots, send, recv), factorise(gram_of(index + 1, gram_group))

    loads[0].wait()
    centre[...] = 2.0 * frequency[...]
    scale[...] = 1.0 / jnp.sqrt(centre[...] * (1.0 - frequency[...]))
    loads[1].wait()
    total, shift = jnp.zeros((2 * BLOCK, ROWS), F32), jnp.zeros((BLOCK, 1), F32)
    start_gram = jnp.zeros((BLOCK, BLOCK), F32)
    for i in range(LOADS):
        columns = slice(i * step, (i + 1) * step)
        narrow = start_block[:, columns].astype(BF16)
        start_gram = start_gram + nt(narrow, narrow)
        terms, shifted = scaled_terms(narrow.astype(F32), i * step // UNIT)
        shift = shift + shifted
        loads[i + 2].wait()
        total = total + nt(terms, g[:, columns])
    slots = p_narrow.at[0]
    slots[var] = sample_product(total, shift).astype(BF16)
    pl.semaphore_wait(barrier, len(everyone))
    pl.semaphore_signal(opposite_sem, 1, device_id=far_peers[1][1], device_id_type=MESH)
    for _, device in along_x:
        pl.semaphore_signal(diagonal_sem, 1, device_id=device, device_id_type=MESH)
    group = exchange(slots, pair_send.at[0], pair_recv.at[0])
    start_group = exchange_gram(0, start_gram)
    for i in range(LOADS):
        g_t[i * step : (i + 1) * step, :] = g[:, i * step : (i + 1) * step].T

    def factorise_start():
        start_inverse[...] = factorise(gram_of(0, start_group))[1]

    wait(group)
    arriving = variant_pass(0, total_of(slots, N_VAR), factorise_start)

    group, (lower, inverse) = sample_pass(0, arriving, p_wide, pair_send.at[1], pair_recv.at[1])
    relative = full(start_inverse[:, 0:BLOCK], lower[:, 0:BLOCK])
    expected = lax.dot_general(
        relative, relative, (((0,), (0,)), ((), ())), precision=lax.Precision.HIGHEST, preferred_element_type=F32
    )
    mixing = decorrelated(expected, inverse)[:, 0:BLOCK]
    wait(group)
    arriving = variant_pass(1, full(mixing, total_of(p_wide, N_VAR)), lambda: None)

    slots = p_narrow.at[1]
    group, (_, inverse) = sample_pass(1, arriving, slots, pair_send.at[2], pair_recv.at[2])
    inverse = inverse[:, 0:BLOCK]
    scaled = inverse * jnp.sqrt(jnp.float32(VARIANTS))
    piece = whole_2.shape[-1]
    for b in range(0, PARTS[1] * NEAR, 4):
        block = jnp.concatenate([whole_2[b // NEAR, b % NEAR + i].astype(F32) for i in range(4)], axis=1)
        load_ref[:, b * piece : (b + 4) * piece] = full(scaled, block)
    wait(group)
    score_ref[...] = full(inverse, total_of(slots, N_VAR))
    for _, out, _ in sent:
        out.wait_send()


def local(genotypes, frequency, start_block):
    row = (COLS // UNIT, 1, UNIT)
    scratch = [
        pltpu.VMEM((ROWS, COLS), BF16),
        pltpu.VMEM((COLS, ROWS), BF16),
        pltpu.VMEM((BLOCK, COLS), F32),
        pltpu.VMEM(row, F32),
        pltpu.VMEM(row, F32),
        pltpu.VMEM(row, F32),
        pltpu.VMEM((2, N_VAR, BLOCK, ROWS), BF16),
        pltpu.VMEM((N_VAR, BLOCK, ROWS), F32),
        pltpu.VMEM((4 * max(PARTS), BLOCK, 128), F32),
        pltpu.VMEM((3, N_VAR, BLOCK, 128), F32),
        pltpu.VMEM((BLOCK, 128), F32),
    ]
    for parts, wire in zip(PARTS, WIRE):
        scratch += [pltpu.VMEM((parts, n, BLOCK, COLS // NEAR // parts), wire) for n in (NEAR, NEAR, FAR, NEAR)]
    scratch += [pltpu.SemaphoreType.DMA((LOADS + 2,))]
    for n in ((3, N_VAR), (3, N_VAR), (sum(PARTS), NEAR), (sum(PARTS), FAR), (sum(PARTS), NEAR)):
        scratch += [pltpu.SemaphoreType.DMA(n)] * 2
    scratch += [pltpu.SemaphoreType.REGULAR] * 2
    vmem, hbm = pl.BlockSpec(memory_space=pltpu.VMEM), pl.BlockSpec(memory_space=pl.ANY)
    loadings, scores = pl.pallas_call(
        kernel,
        name="subspace",
        out_shape=(pltpu.VMEM((BLOCK, COLS), F32), pltpu.VMEM((BLOCK, ROWS), F32)),
        in_specs=[hbm, hbm, hbm],
        out_specs=(vmem, vmem),
        scratch_shapes=scratch,
        compiler_params=pltpu.CompilerParams(collective_id=0, has_side_effects=True, vmem_limit_bytes=48 << 20),
        cost_estimate=pl.CostEstimate(flops=5 * 2 * ROWS * COLS * BLOCK, bytes_accessed=2 * ROWS * COLS, transcendentals=0),
    )(*(pltpu.with_memory_space_constraint(a, pltpu.HBM) for a in (genotypes, frequency.reshape(row), start_block.T)))
    return loadings.T, scores.T


def solution(mesh):
    return jax.shard_map(
        local,
        mesh=mesh,
        in_specs=(P("samp", "var"), P("var"), P("var", None)),
        out_specs=(P("var", None), P("samp", None)),
        check_vma=False,
    )
```

```python
import jax
import jax.numpy as jnp
from jax import lax
from jax.experimental import pallas as pl
from jax.experimental.pallas import tpu as pltpu
from jax.sharding import PartitionSpec as P

MESH = pl.DeviceIdType.MESH
F32, BF16 = jnp.float32, jnp.bfloat16
BLOCK = 16
VARIANTS = 32768
ROWS, COLS = 512, 4096
N_VAR = 8
NEAR, FAR = 16, 4
PARTS = (2, 1)
WIRE = (F32, BF16)
UNIT = 128
LOADS = 8


def split(a, terms):
    parts, rest = [], a
    for _ in range(terms):
        part = rest.astype(BF16)
        parts.append(part)
        rest = rest - part.astype(F32)
    return parts


def nt(a, b):
    return lax.dot_general(a, b, (((1,), (1,)), ((), ())), preferred_element_type=F32)


def full(a, b):
    return jnp.dot(a, b, precision=lax.Precision.HIGHEST, preferred_element_type=F32)


def row_of(a, k):
    return jnp.broadcast_to(a[k : k + 1, :], a.shape)


def spread(matrix):
    shape = (BLOCK, 128)
    columns = [jnp.broadcast_to(matrix[:, j : j + 1], shape) for j in range(BLOCK)]
    return columns, lax.broadcasted_iota(jnp.int32, shape, 0), lax.broadcasted_iota(jnp.int32, shape, 1)


def factorise(gram):
    columns, row, lane = spread(gram)
    inverse = jnp.where(row == lane, 1.0, 0.0).astype(F32)
    roots, lower = jnp.zeros_like(inverse), jnp.zeros_like(inverse)
    for k in range(BLOCK):
        column = columns[k]
        pivot = row_of(column, k)
        root = 1.0 / jnp.sqrt(pivot)
        factor = jnp.where(row > k, column / pivot, 0.0)
        roots = jnp.where(row == k, root, roots)
        lower = jnp.where((lane == k) & (row >= k), column * root, lower)
        for j in range(k + 1, BLOCK):
            columns[j] = columns[j] - factor * row_of(column, j)
        inverse = inverse - factor * row_of(inverse, k)
    return lower, inverse * roots


def decorrelated(expected, rows):
    columns, row, _ = spread(expected)
    for k in range(BLOCK - 1):
        column = columns[k]
        factor = jnp.where(row > k, column / row_of(column, k), 0.0)
        factor = jnp.where(jnp.abs(factor) <= 8.0, factor, 0.0)
        for j in range(k + 1, BLOCK):
            columns[j] = columns[j] - factor * row_of(column, j)
        rows = rows - factor * row_of(rows, k)
    return rows


def kernel(
    g_hbm, freq_hbm, start_hbm, load_ref, score_ref,
    g, g_t, start_block, frequency, centre, scale,
    p_narrow, p_wide, gram_rows, gram_slots, start_inverse,
    part_1, near_1, far_1, whole_1,
    part_2, near_2, far_2, whole_2,
    load_sems, pair_send, pair_recv, gram_send, gram_recv,
    near_send, near_recv, far_send, far_recv, whole_send, whole_recv, far_sem, diagonal_sem,
):
    samp, var = lax.axis_index("samp"), lax.axis_index("var")
    z, x = lax.div(samp, 4), lax.rem(samp, 4)
    z_far, z_near = lax.div(z, 4), lax.rem(z, 4)
    y, core = lax.div(var, 2), lax.rem(var, 2)
    my_near = z_near * 4 + x

    var_peers = []
    for dy in (2, 1, 3, 0):
        for dc in (0, 1):
            if dy or dc:
                other = lax.rem(y + dy, 4) * 2 + lax.rem(core + dc, 2)
                var_peers.append((other, (samp, other)))
    z_at = [z_near, z_near + 1 - 2 * lax.rem(z_near, 2), lax.rem(z_near + 2, 4), 3 - z_near]
    steps = [(a, b) for a in range(4) for b in range(4) if a or b]
    steps.sort(key=lambda step: -step[0] - (0, 1, 2, 1.6)[step[1]])
    near_peers = []
    for a, b in steps:
        slot = z_at[a] * 4 + lax.rem(x + b, 4)
        near_peers.append((slot, (z_far * 16 + slot, var)))
    far_peers = []
    for d in (2, 1, 3):
        slot = lax.rem(z_far + d, 4)
        far_peers.append((slot, (slot * 16 + my_near, var)))

    barrier = pltpu.get_barrier_semaphore()
    along_x = [near_peers[i] for i, (a, b) in enumerate(steps) if a == 0]
    along_z = [near_peers[i] for i, (a, b) in enumerate(steps) if b == 0]
    everyone = along_z + along_x + var_peers
    for _, device in everyone:
        pl.semaphore_signal(barrier, 1, device_id=device, device_id_type=MESH)

    @pl.when(z_far != 2)
    def _():
        pl.semaphore_signal(barrier, 1, device_id=(2 * NEAR + my_near, var), device_id_type=MESH)


    loads = [
        pltpu.make_async_copy(freq_hbm, frequency, load_sems.at[0]),
        pltpu.make_async_copy(start_hbm, start_block, load_sems.at[1]),
    ]
    step = COLS // LOADS
    for i in range(LOADS):
        columns = pl.ds(i * step, step)
        loads.append(pltpu.make_async_copy(g_hbm.at[:, columns], g.at[:, columns], load_sems.at[i + 2]))
    for load in loads:
        load.start()

    def copies(peers, source, target, mine, send, recv):
        return [
            (
                slot,
                pltpu.make_async_remote_copy(
                    src_ref=source(slot), dst_ref=target.at[mine], send_sem=send.at[slot], recv_sem=recv.at[mine],
                    device_id=device, device_id_type=MESH,
                ),
                pltpu.make_async_remote_copy(
                    src_ref=source(slot), dst_ref=target.at[slot], send_sem=send.at[slot], recv_sem=recv.at[slot],
                    device_id=device, device_id_type=MESH,
                ),
            )
            for slot, device in peers
        ]

    sent = []

    def start(group):
        for _, out, _ in group:
            out.start()
        sent.extend(group)

    def wait(group):
        for _, _, back in group:
            back.wait_recv()

    def units(ref, first, n):
        return jnp.concatenate([ref[first + i] for i in range(n)], axis=1)

    def scaled_terms(block, first):
        n = block.shape[1] // UNIT
        high, low = split(block * units(scale, first, n), 2)
        exact = (high.astype(F32) + low.astype(F32)) * units(centre, first, n)
        return jnp.concatenate([high, low], axis=0), jnp.sum(exact, axis=1, keepdims=True)

    def sample_product(total, shift):
        return total[0:BLOCK] + total[BLOCK:] - shift

    def exchange(slots, send, recv):
        group = copies(var_peers, lambda slot: slots.at[var], slots, var, send, recv)
        start(group)
        return group

    def exchange_gram(index, gram):
        slots = gram_slots.at[index]
        half = BLOCK // 2
        slots[var, :, 0:BLOCK] = gram[0:half]
        slots[var, :, BLOCK : 2 * BLOCK] = gram[half:]
        slots[var, :, 2 * BLOCK :] = jnp.zeros((half, 128 - 2 * BLOCK), F32)
        return exchange(slots, gram_send.at[index], gram_recv.at[index])

    def gram_of(index, group):
        wait(group)
        total = total_of(gram_slots.at[index], N_VAR)
        return jnp.concatenate([total[:, 0:BLOCK], total[:, BLOCK : 2 * BLOCK]], axis=0)

    def total_of(slots, n):
        total = slots[0].astype(F32)
        for i in range(1, n):
            total = total + slots[i].astype(F32)
        return total

    blocks = ((part_1, near_1, far_1, whole_1), (part_2, near_2, far_2, whole_2))
    first_stage = (0, PARTS[0])

    def variant_pass(index, sample_block, meanwhile):
        part, near, far, whole = blocks[index]
        wire = part.dtype
        piece = part.shape[-1]
        chunk = max(piece, 2 * UNIT)
        narrow = sample_block.astype(BF16)
        shift = jnp.sum(narrow.astype(F32), axis=1, keepdims=True)
        groups = []
        for h in range(PARTS[index]):
            stage = first_stage[index] + h
            for b in range(0, NEAR * piece, chunk):
                first = h * NEAR * piece + b
                product = jnp.dot(narrow, g[:, first : first + chunk], preferred_element_type=F32)
                n = chunk // UNIT
                product = (product - shift * units(centre, first // UNIT, n)) * units(scale, first // UNIT, n)
                for i in range(chunk // piece):
                    part[h, b // piece + i] = product[:, i * piece : (i + 1) * piece].astype(wire)
            if stage == 0:
                pl.semaphore_wait(diagonal_sem, len(along_x))
            group = copies(
                near_peers, lambda slot: part.at[h, slot], near.at[h], my_near, near_send.at[stage], near_recv.at[stage]
            )
            start(group)
            groups.append(group)
        meanwhile()
        far_groups = []
        for h, group in enumerate(groups):
            stage = first_stage[index] + h
            total = part[h, my_near].astype(F32)
            for slot, _, back in reversed(group):
                back.wait_recv()
                total = total + near[h, slot].astype(F32)
            far[h, z_far] = total.astype(wire)
            if stage == 0:

                @pl.when(z_far != 2)
                def _():
                    pl.semaphore_wait(far_sem, 1)

            group = copies(far_peers, lambda slot: far.at[h, z_far], far.at[h], z_far, far_send.at[stage], far_recv.at[stage])
            start(group)
            far_groups.append(group)
        groups = []
        for h, group in enumerate(far_groups):
            stage = first_stage[index] + h
            wait(group)
            whole[h, my_near] = total_of(far.at[h], FAR).astype(wire)
            group = copies(
                near_peers, lambda slot: whole.at[h, my_near], whole.at[h], my_near, whole_send.at[stage], whole_recv.at[stage]
            )
            start(group)
            groups.append(group)
        return groups

    def sample_pass(index, arriving, slots, send, recv):
        whole = blocks[index][-1]
        depth = 4 * whole.shape[-1]
        total, shift = jnp.zeros((2 * BLOCK, ROWS), F32), jnp.zeros((BLOCK, 1), F32)
        for h in range(PARTS[index]):
            for a in range(4):
                wait([arriving[h][i] for i, step in enumerate(steps) if step[0] == a])
                block = jnp.concatenate([whole[h, z_at[a] * 4 + i] for i in range(4)], axis=1)
                if whole.dtype == BF16:
                    left = right = block
                else:
                    high, middle, low = split(block, 3)
                    left = jnp.concatenate([high, high, middle, high, low, middle], axis=1)
                    right = jnp.concatenate([high, middle, high, low, high, middle], axis=1)
                place = h * 4 + z_at[a]
                gram_rows[place, :, 0:BLOCK] = nt(left, right)
                terms, shifted = scaled_terms(block.astype(F32), place * (depth // UNIT))
                shift = shift + shifted
                total = total + jnp.dot(
                    terms, g_t[pl.ds(pl.multiple_of(place * depth, depth), depth), :], preferred_element_type=F32
                )
        gram = gram_rows[0, :, 0:BLOCK]
        for i in range(1, 4 * PARTS[index]):
            gram = gram + gram_rows[i, :, 0:BLOCK]
        gram_group = exchange_gram(index + 1, gram)
        slots[var] = sample_product(total, shift).astype(slots.dtype)
        return exchange(slots, send, recv), factorise(gram_of(index + 1, gram_group))

    loads[0].wait()
    centre[...] = 2.0 * frequency[...]
    scale[...] = 1.0 / jnp.sqrt(centre[...] * (1.0 - frequency[...]))
    loads[1].wait()
    total, shift = jnp.zeros((2 * BLOCK, ROWS), F32), jnp.zeros((BLOCK, 1), F32)
    start_gram = jnp.zeros((BLOCK, BLOCK), F32)
    for i in range(LOADS):
        columns = slice(i * step, (i + 1) * step)
        narrow = start_block[:, columns].astype(BF16)
        start_gram = start_gram + nt(narrow, narrow)
        terms, shifted = scaled_terms(narrow.astype(F32), i * step // UNIT)
        shift = shift + shifted
        loads[i + 2].wait()
        total = total + nt(terms, g[:, columns])
    slots = p_narrow.at[0]
    slots[var] = sample_product(total, shift).astype(BF16)

    @pl.when(z_far != 2)
    def _():
        pl.semaphore_wait(barrier, len(everyone))

    @pl.when(z_far == 2)
    def _():
        pl.semaphore_wait(barrier, len(everyone) + len(far_peers))
        for _, device in far_peers:
            pl.semaphore_signal(far_sem, 1, device_id=device, device_id_type=MESH)

    for _, device in along_x:
        pl.semaphore_signal(diagonal_sem, 1, device_id=device, device_id_type=MESH)
    group = exchange(slots, pair_send.at[0], pair_recv.at[0])
    start_group = exchange_gram(0, start_gram)
    for i in range(LOADS):
        g_t[i * step : (i + 1) * step, :] = g[:, i * step : (i + 1) * step].T

    def factorise_start():
        start_inverse[...] = factorise(gram_of(0, start_group))[1]

    wait(group)
    arriving = variant_pass(0, total_of(slots, N_VAR), factorise_start)

    group, (lower, inverse) = sample_pass(0, arriving, p_wide, pair_send.at[1], pair_recv.at[1])
    relative = full(start_inverse[:, 0:BLOCK], lower[:, 0:BLOCK])
    expected = lax.dot_general(
        relative, relative, (((0,), (0,)), ((), ())), precision=lax.Precision.HIGHEST, preferred_element_type=F32
    )
    mixing = decorrelated(expected, inverse)[:, 0:BLOCK]
    wait(group)
    arriving = variant_pass(1, full(mixing, total_of(p_wide, N_VAR)), lambda: None)

    slots = p_narrow.at[1]
    group, (_, inverse) = sample_pass(1, arriving, slots, pair_send.at[2], pair_recv.at[2])
    inverse = inverse[:, 0:BLOCK]
    scaled = jnp.concatenate(split(inverse * jnp.sqrt(jnp.float32(VARIANTS)), 3), axis=0)
    piece = whole_2.shape[-1]
    for b in range(0, PARTS[1] * NEAR, 4):
        block = jnp.concatenate([whole_2[b // NEAR, b % NEAR + i] for i in range(4)], axis=1)
        terms = jnp.dot(scaled, block, preferred_element_type=F32)
        load_ref[:, b * piece : (b + 4) * piece] = (terms[2 * BLOCK :] + terms[BLOCK : 2 * BLOCK]) + terms[0:BLOCK]
    for _, out, _ in sent[: -len(group)]:
        out.wait_send()
    wait(group)
    score_ref[...] = full(inverse, total_of(slots, N_VAR))
    for _, out, _ in group:
        out.wait_send()


def local(genotypes, frequency, start_block):
    row = (COLS // UNIT, 1, UNIT)
    scratch = [
        pltpu.VMEM((ROWS, COLS), BF16),
        pltpu.VMEM((COLS, ROWS), BF16),
        pltpu.VMEM((BLOCK, COLS), F32),
        pltpu.VMEM(row, F32),
        pltpu.VMEM(row, F32),
        pltpu.VMEM(row, F32),
        pltpu.VMEM((2, N_VAR, BLOCK, ROWS), BF16),
        pltpu.VMEM((N_VAR, BLOCK, ROWS), F32),
        pltpu.VMEM((4 * max(PARTS), BLOCK, 128), F32),
        pltpu.VMEM((3, N_VAR, BLOCK // 2, 128), F32),
        pltpu.VMEM((BLOCK, 128), F32),
    ]
    for parts, wire in zip(PARTS, WIRE):
        scratch += [pltpu.VMEM((parts, n, BLOCK, COLS // NEAR // parts), wire) for n in (NEAR, NEAR, FAR, NEAR)]
    scratch += [pltpu.SemaphoreType.DMA((LOADS + 2,))]
    for n in ((3, N_VAR), (3, N_VAR), (sum(PARTS), NEAR), (sum(PARTS), FAR), (sum(PARTS), NEAR)):
        scratch += [pltpu.SemaphoreType.DMA(n)] * 2
    scratch += [pltpu.SemaphoreType.REGULAR] * 2
    vmem, hbm = pl.BlockSpec(memory_space=pltpu.VMEM), pl.BlockSpec(memory_space=pl.ANY)
    loadings, scores = pl.pallas_call(
        kernel,
        name="subspace",
        out_shape=(pltpu.VMEM((BLOCK, COLS), F32), pltpu.VMEM((BLOCK, ROWS), F32)),
        in_specs=[hbm, hbm, hbm],
        out_specs=(vmem, vmem),
        scratch_shapes=scratch,
        compiler_params=pltpu.CompilerParams(collective_id=0, has_side_effects=True, vmem_limit_bytes=48 << 20),
        cost_estimate=pl.CostEstimate(flops=5 * 2 * ROWS * COLS * BLOCK, bytes_accessed=2 * ROWS * COLS, transcendentals=0),
    )(*(pltpu.with_memory_space_constraint(a, pltpu.HBM) for a in (genotypes, frequency.reshape(row), start_block.T)))
    return loadings.T, scores.T


def solution(mesh):
    return jax.shard_map(
        local,
        mesh=mesh,
        in_specs=(P("samp", "var"), P("var"), P("var", None)),
        out_specs=(P("var", None), P("samp", None)),
        check_vma=False,
    )
```
